32 devices in a mesh: expert: 16 (over z, y, x), tensor: 2 (over core).
Axes of the slice: x: 2, y: 2, z: 4, core: 2. Of those that a mesh axis runs over, the one named last changes fastest.
Arguments:
- tokens: bfloat16 [256, 3584], P('expert', 'tensor'), may hold values from -6 to 6
- grad_out: bfloat16 [256, 3584], P('expert', 'tensor'), may hold values from -6 to 6
- gate_weights: bfloat16 [256, 8], P('expert'), may hold values from 0.099609375 to 1
- routing: int32 [256, 8], P('expert'), may hold values from 0 to 15, all different within a row; in each aligned block of 16 rows (0 to 15, 16 to 31, ...) at most 12 rows name the same one
- w_gate: bfloat16 [16, 3584, 1024], P('expert', None, 'tensor'), may hold values from -0.09375 to 0.09375
- w_up: bfloat16 [16, 3584, 1024], P('expert', None, 'tensor'), may hold values from -0.09375 to 0.09375
- w_down: bfloat16 [16, 1024, 3584], P('expert', 'tensor'), may hold values from -0.1875 to 0.1875
Outputs:
- grad_tokens: bfloat16 [256, 3584], P('expert', 'tensor')
- grad_gate: bfloat16 [16, 3584, 1024], P('expert', None, 'tensor')
- grad_up: bfloat16 [16, 3584, 1024], P('expert', None, 'tensor')
The draws below stay inside these ranges and needn't reach their ends.
Inputs may be any that keep to these rules, and one draw needn't show every extreme that they name: `routing`: each row names 8 different experts; within the rows of one device (aligned blocks of 16 rows) no expert is named by more than 12 rows.
All inputs are finite; a program needn't handle non-finite values.
Results may differ from the reference program's by a relative error of at most 0.014.
Values may be sent and summed in bfloat16 or wider, within the bound.
A program may use at most 64 MiB of HBM per device.

```python
import math
import jax
import jax.numpy as jnp
import numpy as np
from jax import lax

D = 3584
FF = 1024
TOP = 8
TOK_DEV = 16
EXPERTS = 16
CAP = 12
SLOTS = 192
TOKENS = 256
N_TENSOR = 2


def block_levels(stream_key, shape, pieces, least, high):
    def one(dim, shards_of):
        steps = jax.random.uniform(jax.random.fold_in(jax.random.fold_in(stream_key, 6), dim), (shards_of,), jnp.float32, least / len(pieces), high / len(pieces))
        return jnp.repeat(jnp.exp(steps), shape[dim] // shards_of).reshape((-1,) + (1,) * (len(shape) - dim - 1))

    factor_of = one(*pieces[0])
    for cut in pieces[1:]:
        factor_of = factor_of * one(*cut)
    return factor_of


def assign_block(rng, own, number, rows, amount, top, limit, slope):
    ranking = jax.random.permutation(rng, amount)
    heavy_load, ordinary = portions_of(amount, rows * top, limit, slope, True), portions_of(amount, rows * top, limit, slope, False)
    places = jnp.arange(amount)

    def named(sizes, turn):
        used = int((sizes > 0).sum())
        fixed = max(1, used // 4)
        shifted = fixed + (places - fixed + turn * (used - fixed)) % max(1, amount - fixed)
        return jnp.zeros((amount,), jnp.int32).at[ranking[jnp.where(places < fixed, places, shifted)]].set(jnp.asarray(sizes, jnp.int32))

    sizes = jnp.where(number % 4 == 0, named(heavy_load, number // 4), named(ordinary, number - number // 4 - 1))
    mixed = jax.random.permutation(jax.random.fold_in(own, 3), amount)
    donor, receiver = mixed[0:amount // 2 * 2:2], mixed[1:amount // 2 * 2:2]
    slack = jnp.minimum(sizes[donor] - 1, limit - sizes[receiver]) // 2
    slack = jnp.where((donor == ranking[0]) | (receiver == ranking[0]) | (sizes[receiver] == 0), 0, jnp.maximum(slack, 0))
    shifted = jax.random.randint(jax.random.fold_in(own, 4), (amount // 2,), 0, 1 << 20) % (slack + 1)
    sizes = sizes.at[donor].add(-shifted).at[receiver].add(shifted)
    members = jnp.searchsorted(jnp.cumsum(sizes), jnp.arange(rows * top), side="right").astype(jnp.int32)
    grid = members.reshape(top, rows).T
    grid = grid[jax.random.permutation(jax.random.fold_in(own, 1), rows)]
    turn = jax.random.randint(jax.random.fold_in(own, 2), (rows, 1), 0, top)
    return jnp.take_along_axis(grid, (jnp.arange(top)[None, :] + turn) % top, axis=1)


def portions_of(amount, total, reach, lean, full):
    weights = [(1 << 20) // math.isqrt(standing ** lean) + 1 for standing in range(1, amount + 1)]
    largest = reach if full else min(reach, max(-(-total // amount), total * weights[0] // sum(weights)))
    least = 1 if total - largest >= amount - 1 else 0
    given, surplus = [largest] + [least] * (amount - 1), total - largest - least * (amount - 1)
    while surplus > 0:
        free = [i for i in range(1, amount) if given[i] < largest] or [i for i in range(1, amount) if given[i] < reach]
        pool, budget = sum([weights[i] for i in free]), surplus
        for i in free:
            extra = min(reach - given[i], max(1, budget * weights[i] // pool), surplus)
            given[i] = given[i] + extra
            surplus = surplus - extra
    return np.array(given)


def bell_draw(own_key, dims, width, most, split=(), kind=jnp.bfloat16):
    drawn = jax.random.normal(own_key, dims, jnp.float32) * width
    if len(split) > 0:
        drawn = block_levels(own_key, dims, split, -0.22, 0.18) * drawn
    return jnp.clip(drawn, min=-most, max=most).astype(kind)


def setup_inputs(seed: int = 0) -> dict:
    seeds = jax.random.split(jax.random.key(seed), 8)
    tokens = bell_draw(seeds[0], (TOKENS, D), 1.0, 6.0, ((0, 16), (1, 2)))
    grad_out = bell_draw(seeds[1], (TOKENS, D), 1.0, 6.0, ((0, 16), (1, 2)))
    gate_weights = jnp.clip(0.099609375 + 0.9003906 * jax.random.uniform(seeds[2], (TOKENS, TOP), jnp.float32) ** block_levels(seeds[2], (TOKENS, TOP), ((0, 16),), -0.2, 0.2), 0.099609375, 1.0).astype(jnp.bfloat16)
    routing_keys = jax.random.split(jax.random.fold_in(seeds[3], 1), TOKENS // TOK_DEV)
    routing_turns = jax.random.permutation(jax.random.fold_in(seeds[3], 3), TOKENS // TOK_DEV)
    routing = jax.vmap(lambda own, number: assign_block(jax.random.fold_in(seeds[3], 2), own, number, TOK_DEV, EXPERTS, TOP, CAP, 2))(routing_keys, routing_turns).reshape((TOKENS, TOP))
    w_gate = bell_draw(seeds[4], (EXPERTS, D, FF), D ** -0.5, 0.09375, ((0, 16), (2, 2)))
    w_up = bell_draw(seeds[5], (EXPERTS, D, FF), D ** -0.5, 0.09375, ((0, 16), (2, 2)))
    w_down = bell_draw(seeds[6], (EXPERTS, FF, D), FF ** -0.5, 0.1875, ((0, 16), (1, 2)))
    return {"tokens": tokens, "grad_out": grad_out, "gate_weights": gate_weights, "routing": routing, "w_gate": w_gate, "w_up": w_up, "w_down": w_down}


def expert_step(carry, expert_id, tokens, grad_out, gate_weights, routing, w_gate, w_up, w_down):
    hit = routing == expert_id
    picked = jnp.any(hit, axis=1)
    weight = jnp.sum(jnp.where(hit, gate_weights.astype(jnp.float32), jnp.float32(0.0)), axis=1)
    sort_keys = jnp.where(picked, 0, 1).astype(jnp.int32)
    order = jnp.argsort(sort_keys, stable=True)[:SLOTS].astype(jnp.int32)
    valid = picked[order]
    rows_x = tokens[order]
    rows_dy = grad_out[order]
    scale = jnp.where(valid, weight[order], jnp.float32(0.0))
    wg = w_gate[expert_id]
    wu = w_up[expert_id]
    wd = w_down[expert_id]
    pre_gate = jnp.dot(rows_x, wg, preferred_element_type=jnp.float32)
    pre_up = jnp.dot(rows_x, wu, preferred_element_type=jnp.float32)
    back_act = jnp.dot(rows_dy, wd.T, preferred_element_type=jnp.float32)
    sig = jax.nn.sigmoid(pre_gate)
    d_gate = (scale[:, None] * back_act * pre_up * sig * (1.0 + pre_gate * (1.0 - sig))).astype(jnp.bfloat16)
    d_up = (scale[:, None] * back_act * pre_gate * sig).astype(jnp.bfloat16)
    grad_g = jnp.dot(rows_x.T, d_gate, preferred_element_type=jnp.float32).astype(jnp.bfloat16)
    grad_u = jnp.dot(rows_x.T, d_up, preferred_element_type=jnp.float32).astype(jnp.bfloat16)
    hidden = FF // N_TENSOR
    dg32 = d_gate.astype(jnp.float32).reshape(SLOTS, N_TENSOR, hidden)
    du32 = d_up.astype(jnp.float32).reshape(SLOTS, N_TENSOR, hidden)
    wg32 = wg.astype(jnp.float32).reshape(D, N_TENSOR, hidden)
    wu32 = wu.astype(jnp.float32).reshape(D, N_TENSOR, hidden)
    parts = jnp.einsum('rnh,dnh->nrd', dg32, wg32) + jnp.einsum('rnh,dnh->nrd', du32, wu32)
    rounded = lax.optimization_barrier(parts.astype(jnp.bfloat16)).astype(jnp.float32)
    contrib = jnp.sum(rounded, axis=0) * valid[:, None].astype(jnp.float32)
    carry = carry.at[order].add(contrib)
    return carry, (grad_g, grad_u)


def reference(tokens, grad_out, gate_weights, routing, w_gate, w_up, w_down):
    def step(carry, expert_id):
        return expert_step(carry, expert_id, tokens, grad_out, gate_weights, routing, w_gate, w_up, w_down)

    start = jnp.zeros((TOKENS, D), jnp.float32)
    total, grads = lax.scan(step, start, jnp.arange(EXPERTS, dtype=jnp.int32))
    return total.astype(jnp.bfloat16), grads[0], grads[1]
```

```python
import functools
import jax
import jax.numpy as jnp
from jax import lax
from jax.experimental import pallas as pl
from jax.experimental.pallas import tpu as pltpu
from jax.sharding import PartitionSpec as P

LANES = 128
TILE = 256


def contract_first(left, right):
    return lax.dot_general(
        left, right, (((0,), (0,)), ((), ())), preferred_element_type=jnp.float32
    )


def contract_last(left, right):
    return lax.dot_general(
        left, right, (((1,), (1,)), ((), ())), preferred_element_type=jnp.float32
    )


def act_grads(scale, back_act, pre_gate, pre_up):
    sig = jax.nn.sigmoid(pre_gate)
    d_gate = scale * back_act * pre_up * sig * (1.0 + pre_gate * (1.0 - sig))
    d_up = scale * back_act * pre_gate * sig
    return d_gate.astype(jnp.bfloat16), d_up.astype(jnp.bfloat16)


def kernel(
    tok, gro, gw, rt, wg_hbm, wu_hbm, wd_hbm,
    gt_out, x_out, dg, du,
    x_buf, dy_buf, wg, wu, wd, pre_g, pre_u, part_out, part_in, acc, r2, r1, rz,
    w_sem, xo_sem, z_s, z_r, p1_s, p1_r, p2_s, p2_r, pe_s, pe_r,
    rpe_s, rpe_r, r2_s, r2_r, r1_s, r1_r, rz_s, rz_r,
):
    e = lax.axis_index("expert")
    c = lax.axis_index("tensor")
    rows, half = tok.shape
    total = x_buf.shape[1]
    hidden = wg.shape[1]
    z, y, x = e // 4, (e // 2) % 2, e % 2
    flip_y, flip_x = 2 * (1 - 2 * y), 1 - 2 * x
    flip1 = (1 - c) * flip_y + c * flip_x
    flip2 = (1 - c) * flip_x + c * flip_y
    other1 = c * flip_y + (1 - c) * flip_x
    other2 = c * flip_x + (1 - c) * flip_y
    peer = (e, 1 - c)
    part1 = (e + flip1, c)
    part2 = (e + flip2, c)

    def column(k):
        return lax.rem(z + k, 4) * 4 + 2 * y + x

    def at(owner):
        return pl.ds(pl.multiple_of(owner * rows, 16), rows)

    weights = [
        pltpu.make_async_copy(src, dst, w_sem.at[i])
        for i, (src, dst) in enumerate(((wg_hbm, wg), (wu_hbm, wu), (wd_hbm, wd)))
    ]
    for copy in weights:
        copy.start()

    barrier = pltpu.get_barrier_semaphore()
    for device in [(column(k), c) for k in (1, 2, 3)] + [part1, part2, peer]:
        pl.semaphore_signal(barrier, inc=1, device_id=device, device_id_type=pl.DeviceIdType.MESH)

    picks = rt[...]
    gates = gw[...].astype(jnp.float32)
    lane = lax.broadcasted_iota(jnp.int32, (rows, LANES), 1)
    table = jnp.zeros((rows, LANES), jnp.float32)
    for k in range(picks.shape[1]):
        table += jnp.where(lane == picks[:, k : k + 1], gates[:, k : k + 1], 0.0)
    x_buf[c, at(e), 0:half] = tok[...]
    x_buf[c, at(e), half : half + LANES] = table.astype(jnp.bfloat16)
    dy_buf[c, at(e), :] = gro[...]
    pl.semaphore_wait(barrier, 6)

    bufs = (x_buf, dy_buf)
    sent = []

    def remote(src, dst, send_sem, recv_sem, device):
        return pltpu.make_async_remote_copy(
            src_ref=src, dst_ref=dst, send_sem=send_sem, recv_sem=recv_sem,
            device_id=device, device_id_type=pl.DeviceIdType.MESH,
        )

    def chunk_copy(kind, owner, core, sems, idx, device):
        ref = bufs[kind].at[core, at(owner), :]
        return remote(ref, ref, sems[0].at[kind, idx], sems[1].at[kind, idx], device)

    def go(copy):
        copy.start()
        sent.append(copy)

    zs, p1, p2, pe = (z_s, z_r), (p1_s, p1_r), (p2_s, p2_r), (pe_s, pe_r)

    def to_peer(kind, k, a, b):
        owner = column(k) + a * flip1 + b * flip2
        go(chunk_copy(kind, owner, c, pe, k * 4 + a * 2 + b, peer))

    def to_part2(kind, k, a):
        go(chunk_copy(kind, column(k) + a * flip1, c, p2, k * 2 + a, part2))

    def to_part1(kind, k):
        go(chunk_copy(kind, column(k), c, p1, k, part1))

    def own(kind):
        for k in (2, 1, 3):
            go(chunk_copy(kind, e, c, zs, k - 1, (column(k), c)))
        to_part1(kind, 0)
        to_part2(kind, 0, 0)
        to_peer(kind, 0, 0, 0)

    def from_column(kind, k):
        chunk_copy(kind, column(k), c, zs, 3 - k, (column(k), c)).wait_recv()
        to_part1(kind, k)
        to_part2(kind, k, 0)
        to_peer(kind, k, 0, 0)

    def from_part1(kind, k):
        chunk_copy(kind, column(k) + flip1, c, p1, k, part1).wait_recv()
        to_part2(kind, k, 1)
        to_peer(kind, k, 1, 0)

    def from_part2(kind, k, a):
        owner = column(k) + a * flip1 + flip2
        chunk_copy(kind, owner, c, p2, k * 2 + a, part2).wait_recv()
        to_peer(kind, k, a, 1)

    def from_peer(kind):
        for k in range(4):
            for a in range(2):
                for b in range(2):
                    owner = column(k) + a * other1 + b * other2
                    chunk_copy(kind, owner, 1 - c, pe, k * 4 + a * 2 + b, peer).wait_recv()

    def pre(weight, out, n):
        cols = pl.ds(n * TILE, TILE)
        out[:, cols] = jnp.dot(
            x_buf[0, :, 0:half], weight[0:half, cols], preferred_element_type=jnp.float32
        ) + jnp.dot(
            x_buf[1, :, 0:half], weight[half : 2 * half, cols], preferred_element_type=jnp.float32
        )

    own(0)
    from_part1(0, 0)
    from_column(0, 1)
    from_column(0, 3)
    from_part2(0, 0, 0)
    from_column(0, 2)
    own(1)
    from_part1(0, 1)
    from_part2(0, 0, 1)
    from_part1(0, 3)
    from_part1(0, 2)
    from_part2(0, 1, 0)
    from_part1(1, 0)
    from_part2(0, 1, 1)
    from_column(1, 1)
    from_part2(0, 3, 0)
    from_column(1, 3)
    from_part2(0, 3, 1)
    from_part2(0, 2, 0)
    from_part2(0, 2, 1)
    from_column(1, 2)
    from_part2(1, 0, 0)
    from_peer(0)
    x_copies = [
        pltpu.make_async_copy(
            x_buf.at[h, :, 0:half], x_out.at[:, h * half : (h + 1) * half], xo_sem.at[h]
        )
        for h in range(2)
    ]
    for copy in x_copies:
        copy.start()
    work = [(weight, out, n) for weight, out in ((wg, pre_g), (wu, pre_u)) for n in range(hidden // TILE)]
    rest = [
        functools.partial(from_part1, 1, 1),
        functools.partial(from_part2, 1, 0, 1),
        functools.partial(from_part1, 1, 3),
        functools.partial(from_part1, 1, 2),
        functools.partial(from_part2, 1, 1, 0),
        functools.partial(from_part2, 1, 1, 1),
        functools.partial(from_part2, 1, 3, 0),
        functools.partial(from_part2, 1, 3, 1),
        functools.partial(from_part2, 1, 2, 0),
        functools.partial(from_part2, 1, 2, 1),
    ]
    weights[0].wait()
    weights[1].wait()
    for i, event in enumerate(rest):
        event()
        if 0 < i <= len(work):
            pre(*work[i - 1])
    for item in work[len(rest) - 1 :]:
        pre(*item)
    lanes = lax.broadcasted_iota(jnp.int32, (total, LANES), 1)
    scale = jnp.sum(
        jnp.where(lanes == e, x_buf[0, :, half : half + LANES].astype(jnp.float32), 0.0),
        axis=1, keepdims=True,
    )
    weights[2].wait()
    from_peer(1)
    for n in range(hidden // TILE):
        cols = pl.ds(n * TILE, TILE)
        back = contract_last(dy_buf[0], wd[cols, 0:half]) + contract_last(
            dy_buf[1], wd[cols, half : 2 * half]
        )
        one, two = act_grads(scale, back, pre_g[:, cols], pre_u[:, cols])
        dg[:, cols] = one
        du[:, cols] = two

    def partial(core, n):
        place = pl.ds(pl.multiple_of(core * half + n * TILE, TILE), TILE)
        return contract_last(dg[...], wg[place, :]) + contract_last(du[...], wu[place, :])

    tiles = half // TILE
    for n in range(tiles):
        cols = pl.ds(n * TILE, TILE)
        part_out[:, cols] = partial(1 - c, n).astype(jnp.bfloat16)
        go(remote(part_out.at[:, cols], part_in.at[:, cols], rpe_s.at[n], rpe_r.at[n], peer))
    for n in range(tiles):
        cols = pl.ds(n * TILE, TILE)
        mine = partial(c, n)
        remote(part_out.at[:, cols], part_in.at[:, cols], rpe_s.at[n], rpe_r.at[n], peer).wait_recv()
        acc[:, cols] = (mine + part_in[:, cols].astype(jnp.float32)).astype(jnp.bfloat16)

    def add(owner, ref):
        acc[at(owner), :] = (
            acc[at(owner), :].astype(jnp.float32) + ref[...].astype(jnp.float32)
        ).astype(jnp.bfloat16)

    order = (2, 1, 3, 0)

    def second(k, a, owner):
        idx = k * 2 + a
        return remote(acc.at[at(owner), :], r2.at[idx], r2_s.at[idx], r2_r.at[idx], part2)

    def first(k, owner):
        return remote(acc.at[at(owner), :], r1.at[k], r1_s.at[k], r1_r.at[k], part1)

    def third(k, device):
        return remote(acc.at[at(column(k)), :], rz.at[k - 1], rz_s.at[k - 1], rz_r.at[k - 1], device)

    for k in order:
        for a in (1, 0):
            go(second(k, a, column(k) + a * flip1 + flip2))
    for k in order:
        for a in (1, 0):
            second(k, a, column(k) + a * flip1 + flip2).wait_recv()
            add(column(k) + a * flip1, r2.at[k * 2 + a])
            if a == 1:
                go(first(k, column(k) + flip1))
    for k in order:
        first(k, column(k) + flip1).wait_recv()
        add(column(k), r1.at[k])
        if k:
            go(third(k, (column(k), c)))
    result = acc[at(e), :].astype(jnp.float32)
    for k in (1, 2, 3):
        third(k, (column(k), c)).wait_recv()
        result += rz[k - 1].astype(jnp.float32)
    gt_out[...] = result.astype(jnp.bfloat16)
    for copy in x_copies:
        copy.wait()
    for copy in sent:
        copy.wait_send()


def fused(tokens, grad_out, gate_weights, routing, w_gate, w_up, w_down):
    experts = lax.axis_size("expert")
    rows, half = tokens.shape
    total = experts * rows
    width, hidden = w_gate.shape[1:]
    vmem = pl.BlockSpec(memory_space=pltpu.VMEM)
    hbm = pl.BlockSpec(memory_space=pl.ANY)
    bf16 = jnp.bfloat16
    dma = pltpu.SemaphoreType.DMA
    tiles = half // TILE
    grad_tokens, rows_x, d_gate, d_up = pl.pallas_call(
        kernel,
        out_shape=(
            jax.ShapeDtypeStruct((rows, half), bf16),
            jax.ShapeDtypeStruct((total, width), bf16),
            jax.ShapeDtypeStruct((total, hidden), bf16),
            jax.ShapeDtypeStruct((total, hidden), bf16),
        ),
        in_specs=[vmem] * 4 + [hbm] * 3,
        out_specs=(vmem, hbm, vmem, vmem),
        scratch_shapes=[
            pltpu.VMEM((2, total, half + LANES), bf16),
            pltpu.VMEM((2, total, half), bf16),
            pltpu.VMEM((width, hidden), bf16),
            pltpu.VMEM((width, hidden), bf16),
            pltpu.VMEM((hidden, width), bf16),
            pltpu.VMEM((total, hidden), jnp.float32),
            pltpu.VMEM((total, hidden), jnp.float32),
            pltpu.VMEM((total, half), bf16),
            pltpu.VMEM((total, half), bf16),
            pltpu.VMEM((total, half), bf16),
            pltpu.VMEM((8, rows, half), bf16),
            pltpu.VMEM((4, rows, half), bf16),
            pltpu.VMEM((3, rows, half), bf16),
            dma((3,)), dma((2,)),
            dma((2, 3)), dma((2, 3)), dma((2, 4)), dma((2, 4)),
            dma((2, 8)), dma((2, 8)), dma((2, 16)), dma((2, 16)),
            dma((tiles,)), dma((tiles,)), dma((8,)), dma((8,)),
            dma((4,)), dma((4,)), dma((3,)), dma((3,)),
        ],
        compiler_params=pltpu.CompilerParams(
            collective_id=0, has_side_effects=True, vmem_limit_bytes=60 << 20
        ),
        cost_estimate=pl.CostEstimate(
            flops=10 * total * width * hidden, bytes_accessed=6 * width * hidden, transcendentals=0
        ),
        name="gather_grads_scatter",
    )(tokens, grad_out, gate_weights, routing, w_gate[0], w_up[0], w_down[0])
    grad_g = contract_first(rows_x, d_gate).astype(bf16)[None]
    grad_u = contract_first(rows_x, d_up).astype(bf16)[None]
    return (grad_tokens, grad_g, grad_u)


def dense(tokens, grad_out, gate_weights, routing, w_gate, w_up, w_down):
    me = lax.axis_index("expert")
    weight = jnp.sum(
        jnp.where(
            routing[:, None, :] == jnp.arange(lax.axis_size("expert"))[None, :, None],
            gate_weights[:, None, :],
            jnp.bfloat16(0),
        ).astype(jnp.float32),
        axis=2,
    ).astype(jnp.bfloat16)
    both = jnp.stack([tokens, grad_out])
    got = lax.all_gather(both, "expert", axis=1, tiled=True)
    got = lax.all_gather(got, "tensor", axis=2, tiled=True)
    got_weight = lax.all_gather(weight, "expert", axis=0, tiled=True)
    scale = lax.dynamic_slice_in_dim(got_weight, me, 1, axis=1).astype(jnp.float32)
    rows_x, rows_dy = got[0], got[1]
    weight_g, weight_u, weight_d = w_gate[0], w_up[0], w_down[0]
    pre_gate = jnp.dot(rows_x, weight_g, preferred_element_type=jnp.float32)
    pre_up = jnp.dot(rows_x, weight_u, preferred_element_type=jnp.float32)
    back_act = contract_last(rows_dy, weight_d)
    d_gate, d_up = act_grads(scale, back_act, pre_gate, pre_up)
    grad_g = contract_first(rows_x, d_gate).astype(jnp.bfloat16)[None]
    grad_u = contract_first(rows_x, d_up).astype(jnp.bfloat16)[None]
    part = (contract_last(d_gate, weight_g) + contract_last(d_up, weight_u)).astype(jnp.bfloat16)
    part = lax.psum_scatter(part, "tensor", scatter_dimension=1, tiled=True)
    grad_tokens = lax.psum_scatter(part, "expert", scatter_dimension=0, tiled=True)
    return (grad_tokens, grad_g, grad_u)


def solution(mesh):
    placed = (
        P("expert", "tensor"),
        P("expert", "tensor"),
        P("expert", None),
        P("expert", None),
        P("expert", None, "tensor"),
        P("expert", None, "tensor"),
        P("expert", "tensor", None),
    )
    small = mesh.shape["expert"] == 16 and mesh.shape["tensor"] == 2
    return jax.shard_map(
        fused if small else dense,
        mesh=mesh,
        in_specs=placed,
        out_specs=(P("expert", "tensor"), P("expert", None, "tensor"), P("expert", None, "tensor")),
        check_vma=False,
    )
```

```python
import functools
import jax
import jax.numpy as jnp
from jax import lax
from jax.experimental import pallas as pl
from jax.experimental.pallas import tpu as pltpu
from jax.sharding import PartitionSpec as P

LANES = 128
TILE = 256


def contract_first(left, right):
    return lax.dot_general(
        left, right, (((0,), (0,)), ((), ())), preferred_element_type=jnp.float32
    )


def contract_last(left, right):
    return lax.dot_general(
        left, right, (((1,), (1,)), ((), ())), preferred_element_type=jnp.float32
    )


def act_grads(scale, back_act, pre_gate, pre_up):
    sig = jax.nn.sigmoid(pre_gate)
    d_gate = scale * back_act * pre_up * sig * (1.0 + pre_gate * (1.0 - sig))
    d_up = scale * back_act * pre_gate * sig
    return d_gate.astype(jnp.bfloat16), d_up.astype(jnp.bfloat16)


def weight_grads(x_ref, d_ref, gate_ref, up_ref):
    hidden = gate_ref.shape[2]
    both = contract_first(x_ref[...], d_ref[...]).astype(jnp.bfloat16)
    gate_ref[0] = both[:, 0:hidden]
    up_ref[0] = both[:, hidden : 2 * hidden]


def kernel(
    tok, gro, gw, rt, wg_hbm, wu_hbm, wd_hbm,
    gt_out, x_out, d_all,
    x_buf, dy_buf, wgu, wd, pre_all, back_buf, part_out, part_in, acc, r2, r1, rz,
    in_sem, w_sem, xo_sem, z_s, z_r, p1_s, p1_r, p2_s, p2_r, pe_s, pe_r,
    rpe_s, rpe_r, r2_s, r2_r, r1_s, r1_r, rz_s, rz_r,
):
    e = lax.axis_index("expert")
    c = lax.axis_index("tensor")
    rows, half = tok.shape
    total = x_buf.shape[1]
    hidden = wd.shape[0]
    z, y, x = e // 4, (e // 2) % 2, e % 2
    flip_y, flip_x = 2 * (1 - 2 * y), 1 - 2 * x
    flip1 = (1 - c) * flip_y + c * flip_x
    flip2 = (1 - c) * flip_x + c * flip_y
    other1 = c * flip_y + (1 - c) * flip_x
    other2 = c * flip_x + (1 - c) * flip_y
    peer = (e, 1 - c)
    part1 = (e + flip1, c)
    part2 = (e + flip2, c)

    def column(k):
        return lax.rem(z + k, 4) * 4 + 2 * y + x

    def at(owner):
        return pl.ds(pl.multiple_of(owner * rows, 16), rows)

    inputs = [
        pltpu.make_async_copy(src, dst, in_sem.at[i])
        for i, (src, dst) in enumerate(
            (
                (tok, x_buf.at[c, at(e), 0:half]),
                (gro, dy_buf.at[c, at(e), :]),
            )
        )
    ]
    weights = [
        pltpu.make_async_copy(src, dst, w_sem.at[i])
        for i, (src, dst) in enumerate(
            (
                (wg_hbm, wgu.at[:, 0:hidden]),
                (wu_hbm, wgu.at[:, hidden : 2 * hidden]),
                (wd_hbm, wd),
            )
        )
    ]
    for copy in inputs + weights:
        copy.start()

    barrier = pltpu.get_barrier_semaphore()
    for device in [(column(k), c) for k in (1, 2, 3)] + [part1, part2, peer]:
        pl.semaphore_signal(barrier, inc=1, device_id=device, device_id_type=pl.DeviceIdType.MESH)

    picks = rt[...]
    gates = gw[...].astype(jnp.float32)
    expert = lax.broadcasted_iota(jnp.int32, (LANES, rows), 0)
    table = jnp.zeros((LANES, rows), jnp.float32)
    for k in range(picks.shape[0]):
        table += jnp.where(expert == picks[k : k + 1, :], gates[k : k + 1, :], 0.0)
    row = lax.broadcasted_iota(jnp.int32, (rows, rows), 0)
    col = lax.broadcasted_iota(jnp.int32, (rows, rows), 1)
    eye = jnp.where(row == col, 1.0, 0.0).astype(jnp.bfloat16)
    table = contract_last(eye, table.astype(jnp.bfloat16))
    x_buf[c, at(e), half : half + LANES] = table.astype(jnp.bfloat16)
    inputs[0].wait()
    inputs[1].wait()
    pl.semaphore_wait(barrier, 6)

    bufs = (x_buf, dy_buf)
    sent = []

    def remote(src, dst, send_sem, recv_sem, device):
        return pltpu.make_async_remote_copy(
            src_ref=src, dst_ref=dst, send_sem=send_sem, recv_sem=recv_sem,
            device_id=device, device_id_type=pl.DeviceIdType.MESH,
        )

    def chunk_copy(kind, owner, core, sems, idx, device):
        ref = bufs[kind].at[core, at(owner), :]
        return remote(ref, ref, sems[0].at[kind, idx], sems[1].at[kind, idx], device)

    def go(copy):
        copy.start()
        sent.append(copy)

    zs, p1, p2, pe = (z_s, z_r), (p1_s, p1_r), (p2_s, p2_r), (pe_s, pe_r)

    def to_peer(kind, k, a, b):
        owner = column(k) + a * flip1 + b * flip2
        go(chunk_copy(kind, owner, c, pe, k * 4 + a * 2 + b, peer))

    def to_part2(kind, k, a):
        go(chunk_copy(kind, column(k) + a * flip1, c, p2, k * 2 + a, part2))

    def to_part1(kind, k):
        go(chunk_copy(kind, column(k), c, p1, k, part1))

    def own(kind):
        for k in (2, 1, 3):
            go(chunk_copy(kind, e, c, zs, k - 1, (column(k), c)))
        to_part1(kind, 0)
        to_part2(kind, 0, 0)
        to_peer(kind, 0, 0, 0)

    def from_column(kind, k):
        chunk_copy(kind, column(k), c, zs, 3 - k, (column(k), c)).wait_recv()
        to_part1(kind, k)
        to_part2(kind, k, 0)
        to_peer(kind, k, 0, 0)

    def from_part1(kind, k):
        chunk_copy(kind, column(k) + flip1, c, p1, k, part1).wait_recv()
        to_part2(kind, k, 1)
        to_peer(kind, k, 1, 0)

    def from_part2(kind, k, a):
        owner = column(k) + a * flip1 + flip2
        chunk_copy(kind, owner, c, p2, k * 2 + a, part2).wait_recv()
        to_peer(kind, k, a, 1)

    def from_peer(kind):
        for k in range(4):
            for a in range(2):
                for b in range(2):
                    owner = column(k) + a * other1 + b * other2
                    chunk_copy(kind, owner, 1 - c, pe, k * 4 + a * 2 + b, peer).wait_recv()

    def pre(core, n, fresh):
        cols = pl.ds(n * TILE, TILE)
        depth = pl.ds(pl.multiple_of(core * half, TILE), half)
        value = jnp.dot(
            x_buf[core, :, 0:half], wgu[depth, cols], preferred_element_type=jnp.float32
        )
        pre_all[:, cols] = value if fresh else pre_all[:, cols] + value

    own(0)
    from_part1(0, 0)
    from_column(0, 1)
    from_column(0, 3)
    from_part2(0, 0, 0)
    from_column(0, 2)
    own(1)
    from_part1(0, 1)
    from_part2(0, 0, 1)
    from_part1(0, 3)
    from_part1(0, 2)
    from_part2(0, 1, 0)
    from_part1(1, 0)
    from_part2(0, 1, 1)
    from_column(1, 1)
    from_part2(0, 3, 0)
    from_column(1, 3)
    from_part2(0, 3, 1)
    from_part2(0, 2, 0)
    from_part2(0, 2, 1)
    from_column(1, 2)
    from_part1(1, 1)
    from_part2(1, 0, 0)
    blocks = 2 * hidden // TILE
    events = [
        functools.partial(from_part1, 1, 3),
        functools.partial(from_part1, 1, 2),
        functools.partial(from_part2, 1, 0, 1),
        functools.partial(from_part2, 1, 1, 0),
        functools.partial(from_part2, 1, 1, 1),
        functools.partial(from_part2, 1, 3, 0),
        functools.partial(from_part2, 1, 3, 1),
        functools.partial(from_part2, 1, 2, 0),
        functools.partial(from_part2, 1, 2, 1),
    ]
    weights[0].wait()
    weights[1].wait()
    for n in range(blocks):
        pre(c, n, True)
        events[n]()
    from_peer(0)
    x_copies = [
        pltpu.make_async_copy(
            x_buf.at[h, :, 0:half], x_out.at[:, h * half : (h + 1) * half], xo_sem.at[h]
        )
        for h in range(2)
    ]
    for copy in x_copies:
        copy.start()
    for n in range(blocks):
        pre(1 - c, n, False)
        events[blocks + n]()
    for event in events[2 * blocks :]:
        event()
    lanes = lax.broadcasted_iota(jnp.int32, (total, LANES), 1)
    scale = jnp.sum(
        jnp.where(lanes == e, x_buf[0, :, half : half + LANES].astype(jnp.float32), 0.0),
        axis=1, keepdims=True,
    )
    weights[2].wait()

    def back(core, n):
        depth = pl.ds(pl.multiple_of(core * half, TILE), half)
        return contract_last(dy_buf[core], wd[n * TILE : (n + 1) * TILE, depth])

    own_back = [back(c, n) for n in range(hidden // TILE)]
    for n, value in enumerate(own_back):
        back_buf[:, n * TILE : (n + 1) * TILE] = value
    from_peer(1)
    for n in range(hidden // TILE):
        cols = pl.ds(n * TILE, TILE)
        upper = pl.ds(hidden + n * TILE, TILE)
        value = back_buf[:, cols] + back(1 - c, n)
        one, two = act_grads(scale, value, pre_all[:, cols], pre_all[:, upper])
        d_all[:, cols] = one
        d_all[:, upper] = two

    def partial(core, n):
        place = pl.ds(pl.multiple_of(core * half + n * TILE, TILE), TILE)
        return contract_last(d_all[...], wgu[place, :])

    def tile_copy(n):
        cols = pl.ds(n * TILE, TILE)
        return remote(part_out.at[:, cols], part_in.at[:, cols], rpe_s.at[n], rpe_r.at[n], peer)

    def other_tiles(span):
        for n in range(*span):
            part_out[:, pl.ds(n * TILE, TILE)] = partial(1 - c, n).astype(jnp.bfloat16)
            go(tile_copy(n))

    def own_tiles(span):
        for n in range(*span):
            cols = pl.ds(n * TILE, TILE)
            mine = partial(c, n)
            tile_copy(n).wait_recv()
            acc[:, cols] = (mine + part_in[:, cols].astype(jnp.float32)).astype(jnp.bfloat16)

    tiles = half // TILE
    spans = ((0, tiles // 2), (tiles // 2, tiles))
    order = (2, 1, 3, 0)

    def features(g):
        return pl.ds(spans[g][0] * TILE, (spans[g][1] - spans[g][0]) * TILE)

    def add(owner, ref, g):
        cols = features(g)
        acc[at(owner), cols] = (
            acc[at(owner), cols].astype(jnp.float32) + ref[:, cols].astype(jnp.float32)
        ).astype(jnp.bfloat16)

    def hop(owner, slots, i, sems, g, device):
        cols = features(g)
        return remote(
            acc.at[at(owner), cols], slots.at[i, :, cols], sems[0].at[g, i], sems[1].at[g, i], device
        )

    def second(k, a, g):
        return hop(column(k) + a * flip1 + flip2, r2, k * 2 + a, (r2_s, r2_r), g, part2)

    def first(k, g):
        return hop(column(k) + flip1, r1, k, (r1_s, r1_r), g, part1)

    def third(k, g):
        return hop(column(k), rz, k - 1, (rz_s, rz_r), g, (column(k), c))

    def send_second(g):
        for k in order:
            for a in (1, 0):
                go(second(k, a, g))

    def send_first(g):
        for k in order:
            for a in (1, 0):
                second(k, a, g).wait_recv()
                add(column(k) + a * flip1, r2.at[k * 2 + a], g)
                if a == 1:
                    go(first(k, g))

    def send_third(g):
        for k in order:
            first(k, g).wait_recv()
            add(column(k), r1.at[k], g)
            if k:
                go(third(k, g))

    def finish(g):
        cols = features(g)
        result = acc[at(e), cols].astype(jnp.float32)
        for k in (1, 3, 2):
            third(k, g).wait_recv()
            result += rz[k - 1, :, cols].astype(jnp.float32)
        gt_out[:, cols] = result.astype(jnp.bfloat16)

    for g in range(2):
        other_tiles(spans[g])
        own_tiles(spans[g])
        send_second(g)
    for stage in (send_first, send_third, finish):
        for g in range(2):
            stage(g)
    for copy in x_copies:
        copy.wait()
    for copy in sent:
        copy.wait_send()


def fused(tokens, grad_out, gate_weights, routing, w_gate, w_up, w_down):
    experts = lax.axis_size("expert")
    rows, half = tokens.shape
    total = experts * rows
    width, hidden = w_gate.shape[1:]
    vmem = pl.BlockSpec(memory_space=pltpu.VMEM)
    hbm = pl.BlockSpec(memory_space=pl.ANY)
    bf16 = jnp.bfloat16
    dma = pltpu.SemaphoreType.DMA
    tiles = half // TILE
    grad_tokens, rows_x, d_all = pl.pallas_call(
        kernel,
        out_shape=(
            jax.ShapeDtypeStruct((rows, half), bf16),
            jax.ShapeDtypeStruct((total, width), bf16),
            jax.ShapeDtypeStruct((total, 2 * hidden), bf16),
        ),
        in_specs=[hbm] * 2 + [vmem] * 2 + [hbm] * 3,
        out_specs=(vmem, hbm, vmem),
        scratch_shapes=[
            pltpu.VMEM((2, total, half + LANES), bf16),
            pltpu.VMEM((2, total, half), bf16),
            pltpu.VMEM((width, 2 * hidden), bf16),
            pltpu.VMEM((hidden, width), bf16),
            pltpu.VMEM((total, 2 * hidden), jnp.float32),
            pltpu.VMEM((total, hidden), jnp.float32),
            pltpu.VMEM((total, half), bf16),
            pltpu.VMEM((total, half), bf16),
            pltpu.VMEM((total, half), bf16),
            pltpu.VMEM((8, rows, half), bf16),
            pltpu.VMEM((4, rows, half), bf16),
            pltpu.VMEM((3, rows, half), bf16),
            dma((2,)), dma((3,)), dma((2,)),
            dma((2, 3)), dma((2, 3)), dma((2, 4)), dma((2, 4)),
            dma((2, 8)), dma((2, 8)), dma((2, 16)), dma((2, 16)),
            dma((tiles,)), dma((tiles,)), dma((2, 8)), dma((2, 8)),
            dma((2, 4)), dma((2, 4)), dma((2, 3)), dma((2, 3)),
        ],
        compiler_params=pltpu.CompilerParams(
            collective_id=0, has_side_effects=True, vmem_limit_bytes=60 << 20
        ),
        cost_estimate=pl.CostEstimate(
            flops=10 * total * width * hidden, bytes_accessed=6 * width * hidden, transcendentals=0
        ),
        name="gather_grads_scatter",
    )(tokens, grad_out, gate_weights.T, routing.T, w_gate[0], w_up[0], w_down[0])
    block = 2 * TILE
    grads = jax.ShapeDtypeStruct((1, width, hidden), bf16)
    grad_g, grad_u = pl.pallas_call(
        weight_grads,
        grid=(width // block,),
        out_shape=(grads, grads),
        in_specs=[
            pl.BlockSpec((total, block), lambda i: (0, i)),
            pl.BlockSpec((total, 2 * hidden), lambda i: (0, 0)),
        ],
        out_specs=(
            pl.BlockSpec((1, block, hidden), lambda i: (0, i, 0)),
            pl.BlockSpec((1, block, hidden), lambda i: (0, i, 0)),
        ),
        compiler_params=pltpu.CompilerParams(vmem_limit_bytes=60 << 20),
        cost_estimate=pl.CostEstimate(
            flops=4 * total * width * hidden, bytes_accessed=4 * width * hidden, transcendentals=0
        ),
        name="weight_grads",
    )(rows_x, d_all)
    return (grad_tokens, grad_g, grad_u)


def dense(tokens, grad_out, gate_weights, routing, w_gate, w_up, w_down):
    me = lax.axis_index("expert")
    weight = jnp.sum(
        jnp.where(
            routing[:, None, :] == jnp.arange(lax.axis_size("expert"))[None, :, None],
            gate_weights[:, None, :],
            jnp.bfloat16(0),
        ).astype(jnp.float32),
        axis=2,
    ).astype(jnp.bfloat16)
    both = jnp.stack([tokens, grad_out])
    got = lax.all_gather(both, "expert", axis=1, tiled=True)
    got = lax.all_gather(got, "tensor", axis=2, tiled=True)
    got_weight = lax.all_gather(weight, "expert", axis=0, tiled=True)
    scale = lax.dynamic_slice_in_dim(got_weight, me, 1, axis=1).astype(jnp.float32)
    rows_x, rows_dy = got[0], got[1]
    weight_g, weight_u, weight_d = w_gate[0], w_up[0], w_down[0]
    pre_gate = jnp.dot(rows_x, weight_g, preferred_element_type=jnp.float32)
    pre_up = jnp.dot(rows_x, weight_u, preferred_element_type=jnp.float32)
    back_act = contract_last(rows_dy, weight_d)
    d_gate, d_up = act_grads(scale, back_act, pre_gate, pre_up)
    grad_g = contract_first(rows_x, d_gate).astype(jnp.bfloat16)[None]
    grad_u = contract_first(rows_x, d_up).astype(jnp.bfloat16)[None]
    part = (contract_last(d_gate, weight_g) + contract_last(d_up, weight_u)).astype(jnp.bfloat16)
    part = lax.psum_scatter(part, "tensor", scatter_dimension=1, tiled=True)
    grad_tokens = lax.psum_scatter(part, "expert", scatter_dimension=0, tiled=True)
    return (grad_tokens, grad_g, grad_u)


def solution(mesh):
    placed = (
        P("expert", "tensor"),
        P("expert", "tensor"),
        P("expert", None),
        P("expert", None),
        P("expert", None, "tensor"),
        P("expert", None, "tensor"),
        P("expert", "tensor", None),
    )
    small = mesh.shape["expert"] == 16 and mesh.shape["tensor"] == 2
    return jax.shard_map(
        fused if small else dense,
        mesh=mesh,
        in_specs=placed,
        out_specs=(P("expert", "tensor"), P("expert", None, "tensor"), P("expert", None, "tensor")),
        check_vma=False,
    )
```

```python
import functools
import jax
import jax.numpy as jnp
from jax import lax
from jax.experimental import pallas as pl
from jax.experimental.pallas import tpu as pltpu
from jax.sharding import PartitionSpec as P

LANES = 128
TILE = 256


def contract_first(left, right):
    return lax.dot_general(
        left, right, (((0,), (0,)), ((), ())), preferred_element_type=jnp.float32
    )


def contract_last(left, right):
    return lax.dot_general(
        left, right, (((1,), (1,)), ((), ())), preferred_element_type=jnp.float32
    )


def act_grads(scale, back_act, pre_gate, pre_up):
    sig = jax.nn.sigmoid(pre_gate)
    d_gate = scale * back_act * pre_up * sig * (1.0 + pre_gate * (1.0 - sig))
    d_up = scale * back_act * pre_gate * sig
    return d_gate.astype(jnp.bfloat16), d_up.astype(jnp.bfloat16)


def kernel(
    tok, gro, gw, rt, wg_hbm, wu_hbm, wd_hbm,
    gt_out, gate_out, up_out,
    x_buf, dy_buf, d_all, wgu, wd, pre_all, back_buf, part_out, part_in, acc, r2, r1, rz,
    in_sem, w_sem, z_s, z_r, p1_s, p1_r, p2_s, p2_r, pe_s, pe_r,
    rpe_s, rpe_r, r2_s, r2_r, r1_s, r1_r, rz_s, rz_r,
):
    e = lax.axis_index("expert")
    c = lax.axis_index("tensor")
    rows, half = tok.shape
    total = x_buf.shape[1]
    hidden = wd.shape[0]
    z, y, x = e // 4, (e // 2) % 2, e % 2
    flip_y, flip_x = 2 * (1 - 2 * y), 1 - 2 * x
    flip1 = (1 - c) * flip_y + c * flip_x
    flip2 = (1 - c) * flip_x + c * flip_y
    other1 = c * flip_y + (1 - c) * flip_x
    other2 = c * flip_x + (1 - c) * flip_y
    peer = (e, 1 - c)
    part1 = (e + flip1, c)
    part2 = (e + flip2, c)

    def column(k):
        return lax.rem(z + k, 4) * 4 + 2 * y + x

    def at(owner):
        return pl.ds(pl.multiple_of(owner * rows, 16), rows)

    inputs = [
        pltpu.make_async_copy(src, dst, in_sem.at[i])
        for i, (src, dst) in enumerate(
            (
                (tok, x_buf.at[c, at(e), 0:half]),
                (gro, dy_buf.at[c, at(e), :]),
            )
        )
    ]
    weights = [
        pltpu.make_async_copy(src, dst, w_sem.at[i])
        for i, (src, dst) in enumerate(
            (
                (wg_hbm, wgu.at[:, 0:hidden]),
                (wu_hbm, wgu.at[:, hidden : 2 * hidden]),
                (wd_hbm, wd),
            )
        )
    ]
    for copy in inputs + weights:
        copy.start()

    barrier = pltpu.get_barrier_semaphore()
    for device in [(column(k), c) for k in (1, 2, 3)] + [part1, part2, peer]:
        pl.semaphore_signal(barrier, inc=1, device_id=device, device_id_type=pl.DeviceIdType.MESH)

    picks = rt[...]
    gates = gw[...].astype(jnp.float32)
    expert = lax.broadcasted_iota(jnp.int32, (LANES, rows), 0)
    table = jnp.zeros((LANES, rows), jnp.float32)
    for k in range(picks.shape[0]):
        table += jnp.where(expert == picks[k : k + 1, :], gates[k : k + 1, :], 0.0)
    row = lax.broadcasted_iota(jnp.int32, (rows, rows), 0)
    col = lax.broadcasted_iota(jnp.int32, (rows, rows), 1)
    eye = jnp.where(row == col, 1.0, 0.0).astype(jnp.bfloat16)
    table = contract_last(eye, table.astype(jnp.bfloat16))
    x_buf[c, at(e), half : half + LANES] = table.astype(jnp.bfloat16)
    inputs[0].wait()
    inputs[1].wait()
    pl.semaphore_wait(barrier, 6)

    bufs = (x_buf, dy_buf)
    sent = []

    def remote(src, dst, send_sem, recv_sem, device):
        return pltpu.make_async_remote_copy(
            src_ref=src, dst_ref=dst, send_sem=send_sem, recv_sem=recv_sem,
            device_id=device, device_id_type=pl.DeviceIdType.MESH,
        )

    def chunk_copy(kind, owner, core, sems, idx, device):
        ref = bufs[kind].at[core, at(owner), :]
        return remote(ref, ref, sems[0].at[kind, idx], sems[1].at[kind, idx], device)

    def go(copy):
        copy.start()
        sent.append(copy)

    zs, p1, p2, pe = (z_s, z_r), (p1_s, p1_r), (p2_s, p2_r), (pe_s, pe_r)

    def to_peer(kind, k, a, b):
        owner = column(k) + a * flip1 + b * flip2
        go(chunk_copy(kind, owner, c, pe, k * 4 + a * 2 + b, peer))

    def to_part2(kind, k, a):
        go(chunk_copy(kind, column(k) + a * flip1, c, p2, k * 2 + a, part2))

    def to_part1(kind, k):
        go(chunk_copy(kind, column(k), c, p1, k, part1))

    def own(kind):
        for k in (2, 1, 3):
            go(chunk_copy(kind, e, c, zs, k - 1, (column(k), c)))
        to_part1(kind, 0)
        to_part2(kind, 0, 0)
        to_peer(kind, 0, 0, 0)

    def from_column(kind, k):
        chunk_copy(kind, column(k), c, zs, 3 - k, (column(k), c)).wait_recv()
        to_part1(kind, k)
        to_part2(kind, k, 0)
        to_peer(kind, k, 0, 0)

    def from_part1(kind, k):
        chunk_copy(kind, column(k) + flip1, c, p1, k, part1).wait_recv()
        to_part2(kind, k, 1)
        to_peer(kind, k, 1, 0)

    def from_part2(kind, k, a):
        owner = column(k) + a * flip1 + flip2
        chunk_copy(kind, owner, c, p2, k * 2 + a, part2).wait_recv()
        to_peer(kind, k, a, 1)

    def from_peer(kind):
        for k in range(4):
            for a in range(2):
                for b in range(2):
                    owner = column(k) + a * other1 + b * other2
                    chunk_copy(kind, owner, 1 - c, pe, k * 4 + a * 2 + b, peer).wait_recv()

    def pre(core, n, fresh):
        cols = pl.ds(n * TILE, TILE)
        depth = pl.ds(pl.multiple_of(core * half, TILE), half)
        value = jnp.dot(
            x_buf[core, :, 0:half], wgu[depth, cols], preferred_element_type=jnp.float32
        )
        pre_all[:, cols] = value if fresh else pre_all[:, cols] + value

    own(0)
    from_part1(0, 0)
    from_column(0, 1)
    from_column(0, 3)
    from_part2(0, 0, 0)
    from_column(0, 2)
    own(1)
    from_part1(0, 1)
    from_part2(0, 0, 1)
    from_part1(0, 3)
    from_part1(0, 2)
    from_part2(0, 1, 0)
    from_part1(1, 0)
    from_part2(0, 1, 1)
    from_column(1, 1)
    from_part2(0, 3, 0)
    from_column(1, 3)
    from_part2(0, 3, 1)
    from_part2(0, 2, 0)
    from_part2(0, 2, 1)
    from_column(1, 2)
    from_part1(1, 1)
    from_part2(1, 0, 0)
    blocks = 2 * hidden // TILE
    events = [
        functools.partial(from_part1, 1, 3),
        functools.partial(from_part1, 1, 2),
        functools.partial(from_part2, 1, 0, 1),
        functools.partial(from_part2, 1, 1, 0),
        functools.partial(from_part2, 1, 1, 1),
        functools.partial(from_part2, 1, 3, 0),
        functools.partial(from_part2, 1, 3, 1),
        functools.partial(from_part2, 1, 2, 0),
        functools.partial(from_part2, 1, 2, 1),
    ]
    weights[0].wait()
    weights[1].wait()
    for n in range(blocks):
        pre(c, n, True)
        events[n]()
    from_peer(0)
    for n in range(blocks):
        pre(1 - c, n, False)
        events[blocks + n]()
    for event in events[2 * blocks :]:
        event()
    lanes = lax.broadcasted_iota(jnp.int32, (total, LANES), 1)
    scale = jnp.sum(
        jnp.where(lanes == e, x_buf[0, :, half : half + LANES].astype(jnp.float32), 0.0),
        axis=1, keepdims=True,
    )
    weights[2].wait()

    def back(core, n):
        depth = pl.ds(pl.multiple_of(core * half, TILE), half)
        return contract_last(dy_buf[core], wd[n * TILE : (n + 1) * TILE, depth])

    own_back = [back(c, n) for n in range(hidden // TILE)]
    for n, value in enumerate(own_back):
        back_buf[:, n * TILE : (n + 1) * TILE] = value
    from_peer(1)
    for n in range(hidden // TILE):
        cols = pl.ds(n * TILE, TILE)
        upper = pl.ds(hidden + n * TILE, TILE)
        value = back_buf[:, cols] + back(1 - c, n)
        one, two = act_grads(scale, value, pre_all[:, cols], pre_all[:, upper])
        d_all[:, cols] = one
        d_all[:, upper] = two

    def partial(core, n):
        place = pl.ds(pl.multiple_of(core * half + n * TILE, TILE), TILE)
        return contract_last(d_all[...], wgu[place, :])

    def tile_copy(n):
        cols = pl.ds(n * TILE, TILE)
        return remote(part_out.at[:, cols], part_in.at[:, cols], rpe_s.at[n], rpe_r.at[n], peer)

    def other_tiles(span):
        for n in range(*span):
            part_out[:, pl.ds(n * TILE, TILE)] = partial(1 - c, n).astype(jnp.bfloat16)
            go(tile_copy(n))

    def own_tiles(span):
        for n in range(*span):
            cols = pl.ds(n * TILE, TILE)
            mine = partial(c, n)
            tile_copy(n).wait_recv()
            acc[:, cols] = (mine + part_in[:, cols].astype(jnp.float32)).astype(jnp.bfloat16)

    tiles = half // TILE
    spans = ((0, tiles // 2), (tiles // 2, tiles))
    order = (2, 1, 3, 0)

    def features(g):
        return pl.ds(spans[g][0] * TILE, (spans[g][1] - spans[g][0]) * TILE)

    def add(owner, ref, g):
        cols = features(g)
        acc[at(owner), cols] = (
            acc[at(owner), cols].astype(jnp.float32) + ref[:, cols].astype(jnp.float32)
        ).astype(jnp.bfloat16)

    def hop(owner, slots, i, sems, g, device):
        cols = features(g)
        return remote(
            acc.at[at(owner), cols], slots.at[i, :, cols], sems[0].at[g, i], sems[1].at[g, i], device
        )

    def second(k, a, g):
        return hop(column(k) + a * flip1 + flip2, r2, k * 2 + a, (r2_s, r2_r), g, part2)

    def first(k, g):
        return hop(column(k) + flip1, r1, k, (r1_s, r1_r), g, part1)

    def third(k, g):
        return hop(column(k), rz, k - 1, (rz_s, rz_r), g, (column(k), c))

    def send_second(g):
        for k in order:
            for a in (1, 0):
                go(second(k, a, g))

    def send_first(g):
        for k in order:
            for a in (1, 0):
                second(k, a, g).wait_recv()
                add(column(k) + a * flip1, r2.at[k * 2 + a], g)
                if a == 1:
                    go(first(k, g))

    def send_third(g):
        for k in order:
            first(k, g).wait_recv()
            add(column(k), r1.at[k], g)
            if k:
                go(third(k, g))

    def finish(g):
        cols = features(g)
        result = acc[at(e), cols].astype(jnp.float32)
        for k in (1, 3, 2):
            third(k, g).wait_recv()
            result += rz[k - 1, :, cols].astype(jnp.float32)
        gt_out[:, cols] = result.astype(jnp.bfloat16)

    for g in range(2):
        other_tiles(spans[g])
        own_tiles(spans[g])
        send_second(g)
    def weight_grads(first_tile, last_tile):
        for n in range(first_tile, last_tile):
            core, inner = n // tiles, n % tiles
            both = contract_first(
                x_buf[core, :, inner * TILE : (inner + 1) * TILE], d_all[...]
            ).astype(jnp.bfloat16)
            gate_out[0, n * TILE : (n + 1) * TILE, :] = both[:, 0:hidden]
            up_out[0, n * TILE : (n + 1) * TILE, :] = both[:, hidden : 2 * hidden]

    quarter = 2 * tiles // 4
    send_first(0)
    weight_grads(0, quarter)
    send_first(1)
    weight_grads(quarter, 2 * quarter)
    send_third(0)
    weight_grads(2 * quarter, 3 * quarter)
    send_third(1)
    weight_grads(3 * quarter, 2 * tiles)
    finish(0)
    finish(1)
    for copy in sent:
        copy.wait_send()


def fused(tokens, grad_out, gate_weights, routing, w_gate, w_up, w_down):
    experts = lax.axis_size("expert")
    rows, half = tokens.shape
    total = experts * rows
    width, hidden = w_gate.shape[1:]
    vmem = pl.BlockSpec(memory_space=pltpu.VMEM)
    hbm = pl.BlockSpec(memory_space=pltpu.HBM)
    bf16 = jnp.bfloat16
    dma = pltpu.SemaphoreType.DMA
    tiles = half // TILE
    grads = jax.ShapeDtypeStruct((1, width, hidden), bf16)
    return pl.pallas_call(
        kernel,
        out_shape=(
            jax.ShapeDtypeStruct((rows, half), bf16),
            grads,
            grads,
        ),
        in_specs=[hbm] * 2 + [vmem] * 2 + [hbm] * 3,
        out_specs=(vmem, vmem, vmem),
        scratch_shapes=[
            pltpu.VMEM((2, total, half + LANES), bf16),
            pltpu.VMEM((2, total, half), bf16),
            pltpu.VMEM((total, 2 * hidden), bf16),
            pltpu.VMEM((width, 2 * hidden), bf16),
            pltpu.VMEM((hidden, width), bf16),
            pltpu.VMEM((total, 2 * hidden), jnp.float32),
            pltpu.VMEM((total, hidden), jnp.float32),
            pltpu.VMEM((total, half), bf16),
            pltpu.VMEM((total, half), bf16),
            pltpu.VMEM((total, half), bf16),
            pltpu.VMEM((8, rows, half), bf16),
            pltpu.VMEM((4, rows, half), bf16),
            pltpu.VMEM((3, rows, half), bf16),
            dma((2,)), dma((3,)),
            dma((2, 3)), dma((2, 3)), dma((2, 4)), dma((2, 4)),
            dma((2, 8)), dma((2, 8)), dma((2, 16)), dma((2, 16)),
            dma((tiles,)), dma((tiles,)), dma((2, 8)), dma((2, 8)),
            dma((2, 4)), dma((2, 4)), dma((2, 3)), dma((2, 3)),
        ],
        compiler_params=pltpu.CompilerParams(
            collective_id=0, has_side_effects=True, vmem_limit_bytes=45 << 20
        ),
        cost_estimate=pl.CostEstimate(
            flops=14 * total * width * hidden, bytes_accessed=6 * width * hidden, transcendentals=0
        ),
        name="gather_grads_scatter",
    )(tokens, grad_out, gate_weights.T, routing.T, w_gate[0], w_up[0], w_down[0])


def dense(tokens, grad_out, gate_weights, routing, w_gate, w_up, w_down):
    me = lax.axis_index("expert")
    weight = jnp.sum(
        jnp.where(
            routing[:, None, :] == jnp.arange(lax.axis_size("expert"))[None, :, None],
            gate_weights[:, None, :],
            jnp.bfloat16(0),
        ).astype(jnp.float32),
        axis=2,
    ).astype(jnp.bfloat16)
    both = jnp.stack([tokens, grad_out])
    got = lax.all_gather(both, "expert", axis=1, tiled=True)
    got = lax.all_gather(got, "tensor", axis=2, tiled=True)
    got_weight = lax.all_gather(weight, "expert", axis=0, tiled=True)
    scale = lax.dynamic_slice_in_dim(got_weight, me, 1, axis=1).astype(jnp.float32)
    rows_x, rows_dy = got[0], got[1]
    weight_g, weight_u, weight_d = w_gate[0], w_up[0], w_down[0]
    pre_gate = jnp.dot(rows_x, weight_g, preferred_element_type=jnp.float32)
    pre_up = jnp.dot(rows_x, weight_u, preferred_element_type=jnp.float32)
    back_act = contract_last(rows_dy, weight_d)
    d_gate, d_up = act_grads(scale, back_act, pre_gate, pre_up)
    grad_g = contract_first(rows_x, d_gate).astype(jnp.bfloat16)[None]
    grad_u = contract_first(rows_x, d_up).astype(jnp.bfloat16)[None]
    part = (contract_last(d_gate, weight_g) + contract_last(d_up, weight_u)).astype(jnp.bfloat16)
    part = lax.psum_scatter(part, "tensor", scatter_dimension=1, tiled=True)
    grad_tokens = lax.psum_scatter(part, "expert", scatter_dimension=0, tiled=True)
    return (grad_tokens, grad_g, grad_u)


def solution(mesh):
    placed = (
        P("expert", "tensor"),
        P("expert", "tensor"),
        P("expert", None),
        P("expert", None),
        P("expert", None, "tensor"),
        P("expert", None, "tensor"),
        P("expert", "tensor", None),
    )
    small = mesh.shape["expert"] == 16 and mesh.shape["tensor"] == 2
    return jax.shard_map(
        fused if small else dense,
        mesh=mesh,
        in_specs=placed,
        out_specs=(P("expert", "tensor"), P("expert", None, "tensor"), P("expert", None, "tensor")),
        check_vma=False,
    )
```

```python
import functools
import jax
import jax.numpy as jnp
from jax import lax
from jax.experimental import pallas as pl
from jax.experimental.pallas import tpu as pltpu
from jax.sharding import PartitionSpec as P

LANES = 128
TILE = 256


def contract_first(left, right):
    return lax.dot_general(
        left, right, (((0,), (0,)), ((), ())), preferred_element_type=jnp.float32
    )


def contract_last(left, right):
    return lax.dot_general(
        left, right, (((1,), (1,)), ((), ())), preferred_element_type=jnp.float32
    )


def act_grads(scale, back_act, pre_gate, pre_up):
    sig = jax.nn.sigmoid(pre_gate)
    d_gate = scale * back_act * pre_up * sig * (1.0 + pre_gate * (1.0 - sig))
    d_up = scale * back_act * pre_gate * sig
    return d_gate.astype(jnp.bfloat16), d_up.astype(jnp.bfloat16)


def kernel(
    tok, gro, gw, rt, wg_hbm, wu_hbm, wd_hbm,
    gt_out, gate_out, up_out,
    x_buf, dy_buf, d_all, wgu, wd, pre_all, back_buf, part_out, part_in, acc, r2, r1, rz,
    in_sem, w_sem, z_s, z_r, p1_s, p1_r, p2_s, p2_r, pe_s, pe_r,
    rpe_s, rpe_r, r2_s, r2_r, r1_s, r1_r, rz_s, rz_r,
):
    e = lax.axis_index("expert")
    c = lax.axis_index("tensor")
    rows, half = tok.shape
    total = x_buf.shape[1]
    hidden = wd.shape[0]
    z, y, x = e // 4, (e // 2) % 2, e % 2
    flip_y, flip_x = 2 * (1 - 2 * y), 1 - 2 * x
    flip1 = (1 - c) * flip_y + c * flip_x
    flip2 = (1 - c) * flip_x + c * flip_y
    other1 = c * flip_y + (1 - c) * flip_x
    other2 = c * flip_x + (1 - c) * flip_y
    peer = (e, 1 - c)
    part1 = (e + flip1, c)
    part2 = (e + flip2, c)

    def column(k):
        return lax.rem(z + k, 4) * 4 + 2 * y + x

    def at(owner):
        return pl.ds(pl.multiple_of(owner * rows, 16), rows)

    inputs = [
        pltpu.make_async_copy(src, dst, in_sem.at[i])
        for i, (src, dst) in enumerate(
            (
                (tok, x_buf.at[c, at(e), 0:half]),
                (gro, dy_buf.at[c, at(e), :]),
            )
        )
    ]
    weights = [
        pltpu.make_async_copy(src, dst, w_sem.at[i])
        for i, (src, dst) in enumerate(
            (
                (wg_hbm, wgu.at[:, 0:hidden]),
                (wu_hbm, wgu.at[:, hidden : 2 * hidden]),
                (wd_hbm, wd),
            )
        )
    ]
    for copy in inputs + weights:
        copy.start()

    barrier = pltpu.get_barrier_semaphore()
    for device in [(column(k), c) for k in (1, 2, 3)] + [part1, part2, peer]:
        pl.semaphore_signal(barrier, inc=1, device_id=device, device_id_type=pl.DeviceIdType.MESH)

    picks = rt[...]
    gates = gw[...].astype(jnp.float32)
    expert = lax.broadcasted_iota(jnp.int32, (LANES, rows), 0)
    table = jnp.zeros((LANES, rows), jnp.float32)
    for k in range(picks.shape[0]):
        table += jnp.where(expert == picks[k : k + 1, :], gates[k : k + 1, :], 0.0)
    row = lax.broadcasted_iota(jnp.int32, (rows, rows), 0)
    col = lax.broadcasted_iota(jnp.int32, (rows, rows), 1)
    eye = jnp.where(row == col, 1.0, 0.0).astype(jnp.bfloat16)
    table = contract_last(eye, table.astype(jnp.bfloat16))
    x_buf[c, at(e), half : half + LANES] = table.astype(jnp.bfloat16)
    inputs[0].wait()
    inputs[1].wait()
    pl.semaphore_wait(barrier, 6)

    bufs = (x_buf, dy_buf)
    sent = []

    def remote(src, dst, send_sem, recv_sem, device):
        return pltpu.make_async_remote_copy(
            src_ref=src, dst_ref=dst, send_sem=send_sem, recv_sem=recv_sem,
            device_id=device, device_id_type=pl.DeviceIdType.MESH,
        )

    def chunk_copy(kind, owner, core, sems, idx, device):
        ref = bufs[kind].at[core, at(owner), :]
        return remote(ref, ref, sems[0].at[kind, idx], sems[1].at[kind, idx], device)

    def go(copy):
        copy.start()
        sent.append(copy)

    zs, p1, p2, pe = (z_s, z_r), (p1_s, p1_r), (p2_s, p2_r), (pe_s, pe_r)

    def to_peer(kind, k, a, b):
        owner = column(k) + a * flip1 + b * flip2
        go(chunk_copy(kind, owner, c, pe, k * 4 + a * 2 + b, peer))

    def to_part2(kind, k, a):
        go(chunk_copy(kind, column(k) + a * flip1, c, p2, k * 2 + a, part2))

    def to_part1(kind, k):
        go(chunk_copy(kind, column(k), c, p1, k, part1))

    def own_column(kind):
        for k in (2, 1, 3):
            go(chunk_copy(kind, e, c, zs, k - 1, (column(k), c)))

    def own(kind):
        to_part1(kind, 0)
        to_part2(kind, 0, 0)
        to_peer(kind, 0, 0, 0)

    def from_column(kind, k):
        chunk_copy(kind, column(k), c, zs, 3 - k, (column(k), c)).wait_recv()
        to_part1(kind, k)
        to_part2(kind, k, 0)
        to_peer(kind, k, 0, 0)

    def from_part1(kind, k):
        chunk_copy(kind, column(k) + flip1, c, p1, k, part1).wait_recv()
        to_part2(kind, k, 1)
        to_peer(kind, k, 1, 0)

    def from_part2(kind, k, a):
        owner = column(k) + a * flip1 + flip2
        chunk_copy(kind, owner, c, p2, k * 2 + a, part2).wait_recv()
        to_peer(kind, k, a, 1)

    def from_peer(kind):
        for k in range(4):
            for a in range(2):
                for b in range(2):
                    owner = column(k) + a * other1 + b * other2
                    chunk_copy(kind, owner, 1 - c, pe, k * 4 + a * 2 + b, peer).wait_recv()

    def pre(core, n, fresh):
        cols = pl.ds(n * TILE, TILE)
        depth = pl.ds(pl.multiple_of(core * half, TILE), half)
        value = jnp.dot(
            x_buf[core, :, 0:half], wgu[depth, cols], preferred_element_type=jnp.float32
        )
        pre_all[:, cols] = value if fresh else pre_all[:, cols] + value

    own_column(0)
    own(0)
    from_part1(0, 0)
    own_column(1)
    from_column(0, 1)
    from_column(0, 3)
    from_part2(0, 0, 0)
    from_column(0, 2)
    own(1)
    from_part1(0, 1)
    from_part2(0, 0, 1)
    from_part1(0, 3)
    from_part1(0, 2)
    from_part2(0, 1, 0)
    from_part1(1, 0)
    from_part2(0, 1, 1)
    from_column(1, 1)
    from_part2(0, 3, 0)
    from_column(1, 3)
    from_part2(0, 3, 1)
    from_part2(0, 2, 0)
    from_part2(0, 2, 1)
    from_column(1, 2)
    from_part1(1, 1)
    from_part2(1, 0, 0)
    blocks = 2 * hidden // TILE
    events = [
        functools.partial(from_part1, 1, 3),
        functools.partial(from_part1, 1, 2),
        functools.partial(from_part2, 1, 0, 1),
        functools.partial(from_part2, 1, 1, 0),
        functools.partial(from_part2, 1, 1, 1),
        functools.partial(from_part2, 1, 3, 0),
        functools.partial(from_part2, 1, 3, 1),
        functools.partial(from_part2, 1, 2, 0),
        functools.partial(from_part2, 1, 2, 1),
    ]
    weights[0].wait()
    weights[1].wait()
    for n in range(blocks):
        pre(c, n, True)
        events[n]()
    from_peer(0)
    for n in range(blocks):
        pre(1 - c, n, False)
        events[blocks + n]()
    for event in events[2 * blocks :]:
        event()
    lanes = lax.broadcasted_iota(jnp.int32, (total, LANES), 1)
    scale = jnp.sum(
        jnp.where(lanes == e, x_buf[0, :, half : half + LANES].astype(jnp.float32), 0.0),
        axis=1, keepdims=True,
    )
    weights[2].wait()

    def back(core, n):
        depth = pl.ds(pl.multiple_of(core * half, TILE), half)
        return contract_last(dy_buf[core], wd[n * TILE : (n + 1) * TILE, depth])

    own_back = [back(c, n) for n in range(hidden // TILE)]
    for n, value in enumerate(own_back):
        back_buf[:, n * TILE : (n + 1) * TILE] = value
    from_peer(1)
    for n in range(hidden // TILE):
        cols = pl.ds(n * TILE, TILE)
        upper = pl.ds(hidden + n * TILE, TILE)
        value = back_buf[:, cols] + back(1 - c, n)
        one, two = act_grads(scale, value, pre_all[:, cols], pre_all[:, upper])
        d_all[:, cols] = one
        d_all[:, upper] = two

    def partial(core, n):
        place = pl.ds(pl.multiple_of(core * half + n * TILE, TILE), TILE)
        return contract_last(d_all[...], wgu[place, :])

    def tile_copy(n):
        cols = pl.ds(n * TILE, TILE)
        return remote(part_out.at[:, cols], part_in.at[:, cols], rpe_s.at[n], rpe_r.at[n], peer)

    def other_tiles(span):
        for n in range(*span):
            part_out[:, pl.ds(n * TILE, TILE)] = partial(1 - c, n).astype(jnp.bfloat16)
            go(tile_copy(n))

    def own_tiles(span):
        for n in range(*span):
            cols = pl.ds(n * TILE, TILE)
            mine = partial(c, n)
            tile_copy(n).wait_recv()
            acc[:, cols] = (mine + part_in[:, cols].astype(jnp.float32)).astype(jnp.bfloat16)

    tiles = half // TILE
    spans = ((0, tiles // 2), (tiles // 2, tiles))
    order = (2, 1, 3, 0)

    def features(g):
        return pl.ds(spans[g][0] * TILE, (spans[g][1] - spans[g][0]) * TILE)

    def add(owner, ref, g):
        cols = features(g)
        acc[at(owner), cols] = (
            acc[at(owner), cols].astype(jnp.float32) + ref[:, cols].astype(jnp.float32)
        ).astype(jnp.bfloat16)

    def hop(owner, slots, i, sems, g, device):
        cols = features(g)
        return remote(
            acc.at[at(owner), cols], slots.at[i, :, cols], sems[0].at[g, i], sems[1].at[g, i], device
        )

    def second(k, a, g):
        return hop(column(k) + a * flip1 + flip2, r2, k * 2 + a, (r2_s, r2_r), g, part2)

    def first(k, g):
        return hop(column(k) + flip1, r1, k, (r1_s, r1_r), g, part1)

    def third(k, g):
        return hop(column(k), rz, k - 1, (rz_s, rz_r), g, (column(k), c))

    def send_second(g):
        for k in order:
            for a in (1, 0):
                go(second(k, a, g))

    def send_first(g):
        for k in order:
            for a in (1, 0):
                second(k, a, g).wait_recv()
                add(column(k) + a * flip1, r2.at[k * 2 + a], g)
                if a == 1:
                    go(first(k, g))

    def send_third(g):
        for k in order:
            first(k, g).wait_recv()
            add(column(k), r1.at[k], g)
            if k:
                go(third(k, g))

    def finish(g):
        cols = features(g)
        result = acc[at(e), cols].astype(jnp.float32)
        for k in (1, 3, 2):
            third(k, g).wait_recv()
            result += rz[k - 1, :, cols].astype(jnp.float32)
        gt_out[:, cols] = result.astype(jnp.bfloat16)

    for g in range(2):
        other_tiles(spans[g])
        own_tiles(spans[g])
        send_second(g)
    def weight_grads(first_tile, last_tile):
        for n in range(first_tile, last_tile):
            core, inner = n // tiles, n % tiles
            both = contract_first(
                x_buf[core, :, inner * TILE : (inner + 1) * TILE], d_all[...]
            ).astype(jnp.bfloat16)
            gate_out[0, n * TILE : (n + 1) * TILE, :] = both[:, 0:hidden]
            up_out[0, n * TILE : (n + 1) * TILE, :] = both[:, hidden : 2 * hidden]

    quarter = 2 * tiles // 4
    send_first(0)
    weight_grads(0, quarter)
    send_first(1)
    weight_grads(quarter, 2 * quarter)
    send_third(0)
    weight_grads(2 * quarter, 3 * quarter)
    send_third(1)
    weight_grads(3 * quarter, 2 * tiles)
    finish(0)
    finish(1)
    for copy in sent:
        copy.wait_send()


def fused(tokens, grad_out, gate_weights, routing, w_gate, w_up, w_down):
    experts = lax.axis_size("expert")
    rows, half = tokens.shape
    total = experts * rows
    width, hidden = w_gate.shape[1:]
    vmem = pl.BlockSpec(memory_space=pltpu.VMEM)
    hbm = pl.BlockSpec(memory_space=pltpu.HBM)
    bf16 = jnp.bfloat16
    dma = pltpu.SemaphoreType.DMA
    tiles = half // TILE
    grads = jax.ShapeDtypeStruct((1, width, hidden), bf16)
    return pl.pallas_call(
        kernel,
        out_shape=(
            jax.ShapeDtypeStruct((rows, half), bf16),
            grads,
            grads,
        ),
        in_specs=[hbm] * 2 + [vmem] * 2 + [hbm] * 3,
        out_specs=(vmem, vmem, vmem),
        scratch_shapes=[
            pltpu.VMEM((2, total, half + LANES), bf16),
            pltpu.VMEM((2, total, half), bf16),
            pltpu.VMEM((total, 2 * hidden), bf16),
            pltpu.VMEM((width, 2 * hidden), bf16),
            pltpu.VMEM((hidden, width), bf16),
            pltpu.VMEM((total, 2 * hidden), jnp.float32),
            pltpu.VMEM((total, hidden), jnp.float32),
            pltpu.VMEM((total, half), bf16),
            pltpu.VMEM((total, half), bf16),
            pltpu.VMEM((total, half), bf16),
            pltpu.VMEM((8, rows, half), bf16),
            pltpu.VMEM((4, rows, half), bf16),
            pltpu.VMEM((3, rows, half), bf16),
            dma((2,)), dma((3,)),
            dma((2, 3)), dma((2, 3)), dma((2, 4)), dma((2, 4)),
            dma((2, 8)), dma((2, 8)), dma((2, 16)), dma((2, 16)),
            dma((tiles,)), dma((tiles,)), dma((2, 8)), dma((2, 8)),
            dma((2, 4)), dma((2, 4)), dma((2, 3)), dma((2, 3)),
        ],
        compiler_params=pltpu.CompilerParams(
            collective_id=0, has_side_effects=True, vmem_limit_bytes=45 << 20
        ),
        cost_estimate=pl.CostEstimate(
            flops=14 * total * width * hidden, bytes_accessed=6 * width * hidden, transcendentals=0
        ),
        name="gather_grads_scatter",
    )(tokens, grad_out, gate_weights.T, routing.T, w_gate[0], w_up[0], w_down[0])


def dense(tokens, grad_out, gate_weights, routing, w_gate, w_up, w_down):
    me = lax.axis_index("expert")
    weight = jnp.sum(
        jnp.where(
            routing[:, None, :] == jnp.arange(lax.axis_size("expert"))[None, :, None],
            gate_weights[:, None, :],
            jnp.bfloat16(0),
        ).astype(jnp.float32),
        axis=2,
    ).astype(jnp.bfloat16)
    both = jnp.stack([tokens, grad_out])
    got = lax.all_gather(both, "expert", axis=1, tiled=True)
    got = lax.all_gather(got, "tensor", axis=2, tiled=True)
    got_weight = lax.all_gather(weight, "expert", axis=0, tiled=True)
    scale = lax.dynamic_slice_in_dim(got_weight, me, 1, axis=1).astype(jnp.float32)
    rows_x, rows_dy = got[0], got[1]
    weight_g, weight_u, weight_d = w_gate[0], w_up[0], w_down[0]
    pre_gate = jnp.dot(rows_x, weight_g, preferred_element_type=jnp.float32)
    pre_up = jnp.dot(rows_x, weight_u, preferred_element_type=jnp.float32)
    back_act = contract_last(rows_dy, weight_d)
    d_gate, d_up = act_grads(scale, back_act, pre_gate, pre_up)
    grad_g = contract_first(rows_x, d_gate).astype(jnp.bfloat16)[None]
    grad_u = contract_first(rows_x, d_up).astype(jnp.bfloat16)[None]
    part = (contract_last(d_gate, weight_g) + contract_last(d_up, weight_u)).astype(jnp.bfloat16)
    part = lax.psum_scatter(part, "tensor", scatter_dimension=1, tiled=True)
    grad_tokens = lax.psum_scatter(part, "expert", scatter_dimension=0, tiled=True)
    return (grad_tokens, grad_g, grad_u)


def solution(mesh):
    placed = (
        P("expert", "tensor"),
        P("expert", "tensor"),
        P("expert", None),
        P("expert", None),
        P("expert", None, "tensor"),
        P("expert", None, "tensor"),
        P("expert", "tensor", None),
    )
    small = mesh.shape["expert"] == 16 and mesh.shape["tensor"] == 2
    return jax.shard_map(
        fused if small else dense,
        mesh=mesh,
        in_specs=placed,
        out_specs=(P("expert", "tensor"), P("expert", None, "tensor"), P("expert", None, "tensor")),
        check_vma=False,
    )
```
